32 devices in a mesh: pts: 4 (over x, core), snap: 8 (over z, y).
Axes of the slice: x: 2, y: 2, z: 4, core: 2. Of those that a mesh axis runs over, the one named last changes fastest.
Arguments:
- snapshots: bfloat16 [1024, 3, 16384], P('snap', None, 'pts')
- block_starts: int32 [31], replicated, may hold values from 0 to 960, as said below
- point_slab: int32 [16384], P(('pts', 'snap')), may hold values from 0 to 15
- slab_weight: float32 [16], replicated, may hold values from 1 to 10
Outputs:
- mode_field: bfloat16 [2, 33, 31, 3, 16384], P(None, None, None, None, ('pts', 'snap'))
- r_factor: float32 [2, 33, 31, 31], replicated
The draws below stay inside these ranges and needn't reach their ends.
Inputs may be any that keep to these rules, and one draw needn't show every extreme that they name: `block_starts`: strictly increasing; the first is 0 and the last is 960; neighbours lie more than 16 apart.
All inputs are finite; a program needn't handle non-finite values.
Results may differ from the reference program's by a relative error of at most 0.0017.
The reference program's roundings to bfloat16 on the way (of `dft_table`) count: a program that leaves them out, or rounds other values in their place, can miss the bound.
Values may be sent and summed in bfloat16 or wider, within the bound.
A program may use at most 128 MiB of HBM per device.

```python
import math
import jax
import jax.numpy as jnp
from jax import lax

NT = 1024
WIN = 64
NSLAB = 16
HOP = 32
NB = 31
NF = 33
NP = 16384


def draw_snapshots(key, part):
    position = jnp.arange(NP, dtype=jnp.float32) / NP
    time_index = jnp.arange(NT, dtype=jnp.int32)
    top_bits = NT.bit_length() - 1
    noise_key = jax.random.fold_in(key, 11)
    values = 0.6 * jnp.clip(jax.random.normal(noise_key, (NT, 3, NP), jnp.float32), -6.0, 6.0)
    envelope = jnp.exp(0.5 * jnp.log(3.0) * position)
    for wave_index in range(8):
        wave_key = jax.random.fold_in(key, 100 + wave_index)
        key_bits, key_cycle, key_cos, key_sin = jax.random.split(wave_key, 4)
        bit_count = jax.random.randint(key_bits, (), 2, top_bits, dtype=jnp.int32)
        cycle_top = jnp.left_shift(jnp.int32(1), bit_count)
        cycle_count = jax.random.randint(key_cycle, (), 1, cycle_top, dtype=jnp.int32)
        phase_index = cycle_count * time_index % NT
        phase_angle = 2.0 * math.pi / NT * phase_index.astype(jnp.float32)
        bin_value = cycle_count.astype(jnp.float32) * (WIN / NT)
        strength = 1.2 / jnp.sqrt(1.0 + bin_value)
        coef_cos = jax.random.normal(key_cos, (3, NP), jnp.float32)
        coef_sin = jax.random.normal(key_sin, (3, NP), jnp.float32)
        values = values + strength * (jnp.cos(phase_angle)[:, None, None] * coef_cos[None] + jnp.sin(phase_angle)[:, None, None] * coef_sin[None])
    return (values * envelope[None, None, :]).astype(jnp.bfloat16)


def draw_block_starts(key, part):
    index = jnp.arange(NB, dtype=jnp.int32)
    jitter = jax.random.randint(key, (NB,), 0, HOP // 2, dtype=jnp.int32)
    inner = (index > 0) & (index < NB - 1)
    return index * HOP + jnp.where(inner, jitter, jnp.zeros_like(jitter))


def set_ends(array, own_key, low, top_value):
    longest = array.shape.index(max(array.shape))
    spots = []
    for shift in (0, 1):
        where = [jax.random.randint(jax.random.fold_in(own_key, axis), (), 0, length) for axis, length in enumerate(array.shape)]
        where[longest] = (where[longest] + shift) % array.shape[longest]
        spots.append(tuple(where))
    return array.at[spots[0]].set(low).at[spots[1]].set(top_value)


def setup_inputs(seed: int = 0) -> dict:
    splits = jax.random.split(jax.random.key(seed), 5)
    snapshots = draw_snapshots(jax.random.fold_in(splits[4], 71), 0)
    block_starts = draw_block_starts(jax.random.fold_in(splits[4], 71), 0)
    point_slab = set_ends(jax.random.randint(splits[2], (NP,), 0, NSLAB), jax.random.fold_in(splits[2], 1), 0, NSLAB - 1).astype(jnp.int32)
    slab_weight = jnp.clip(jnp.exp(jax.random.uniform(splits[3], (NSLAB,), jnp.float32, math.log(1.0), math.log(10.0))), 1.0, 10.0)
    return dict(snapshots=snapshots, block_starts=block_starts, point_slab=point_slab, slab_weight=slab_weight)


def make_tables(length, freq_count):
    steps_time = jnp.arange(length, dtype=jnp.int32)
    freq_index = jnp.arange(freq_count, dtype=jnp.int32)
    phase_index = freq_index[:, None] * steps_time[None, :] % length
    angle_value = 2.0 * math.pi / length * phase_index.astype(jnp.float32)
    window = 0.5 - 0.5 * jnp.cos(2.0 * math.pi / length * steps_time.astype(jnp.float32))
    dft_table = jnp.stack([window[None, :] * jnp.cos(angle_value), -window[None, :] * jnp.sin(angle_value)]).astype(jnp.bfloat16)
    row_sums = lax.optimization_barrier(jnp.sum(dft_table.astype(jnp.float32), axis=2))
    return (dft_table, row_sums)

def spectra(series, starts, dft_table, row_sums):
    blocks = jax.vmap(lambda offset: lax.dynamic_slice_in_dim(series, offset, WIN, 0))(starts)
    raw_spec = jnp.einsum('kfw,bwcp->kfbcp', dft_table.astype(jnp.float32), blocks.astype(jnp.float32), precision=lax.Precision.HIGHEST)
    time_mean = lax.optimization_barrier(jnp.sum(series.astype(jnp.float32), axis=0)) / NT
    return raw_spec - row_sums[:, :, None, None, None] * time_mean[None, None, None]

def gram(amplitude):
    highest = lax.Precision.HIGHEST
    amp_real, amp_imag = (amplitude[0], amplitude[1])
    part_real = jnp.einsum('fbn,fdn->bdf', amp_real, amp_real, precision=highest) + jnp.einsum('fbn,fdn->bdf', amp_imag, amp_imag, precision=highest)
    part_imag = jnp.einsum('fbn,fdn->bdf', amp_real, amp_imag, precision=highest) - jnp.einsum('fbn,fdn->bdf', amp_imag, amp_real, precision=highest)
    return (part_real, part_imag)

def complex_cholesky(gram_real, gram_imag):
    size_n = gram_real.shape[0]
    positions = jnp.arange(size_n, dtype=jnp.int32)
    rows_real = []
    rows_imag = []
    for column in range(size_n):
        rest_real = gram_real[column]
        rest_imag = gram_imag[column]
        if column > 0:
            done_real = jnp.stack(rows_real)
            done_imag = jnp.stack(rows_imag)
            above_real = done_real[:, column]
            above_imag = done_imag[:, column]
            rest_real = rest_real - lax.optimization_barrier(jnp.sum(above_real[:, None] * done_real + above_imag[:, None] * done_imag, axis=0))
            rest_imag = rest_imag - lax.optimization_barrier(jnp.sum(above_real[:, None] * done_imag - above_imag[:, None] * done_real, axis=0))
        pivot_value = jnp.sqrt(rest_real[column])
        keep_real = (positions >= column)[:, None]
        keep_imag = (positions > column)[:, None]
        rows_real.append(jnp.where(keep_real, rest_real / pivot_value, jnp.zeros_like(rest_real)))
        rows_imag.append(jnp.where(keep_imag, rest_imag / pivot_value, jnp.zeros_like(rest_imag)))
    return (jnp.stack(rows_real), jnp.stack(rows_imag))

def upper_inverse(upper_real, upper_imag):
    size_n = upper_real.shape[0]
    identity = jnp.eye(size_n, dtype=upper_real.dtype)
    rows_real = []
    rows_imag = []
    for row_index in reversed(range(size_n)):
        rest_real = jnp.broadcast_to(identity[row_index][:, None], upper_real.shape[1:])
        rest_imag = jnp.zeros_like(rest_real)
        if row_index < size_n - 1:
            done_real = jnp.stack(rows_real[::-1])
            done_imag = jnp.stack(rows_imag[::-1])
            coef_real = upper_real[row_index, row_index + 1:]
            coef_imag = upper_imag[row_index, row_index + 1:]
            rest_real = rest_real - lax.optimization_barrier(jnp.sum(coef_real[:, None] * done_real - coef_imag[:, None] * done_imag, axis=0))
            rest_imag = rest_imag - lax.optimization_barrier(jnp.sum(coef_real[:, None] * done_imag + coef_imag[:, None] * done_real, axis=0))
        pivot_value = upper_real[row_index, row_index]
        rows_real.append(rest_real / pivot_value)
        rows_imag.append(rest_imag / pivot_value)
    return (jnp.stack(rows_real[::-1]), jnp.stack(rows_imag[::-1]))

def project(amplitude, inv_real, inv_imag):
    highest = lax.Precision.HIGHEST
    amp_real, amp_imag = (amplitude[0], amplitude[1])
    mode_real = jnp.einsum('fbn,bmf->fmn', amp_real, inv_real, precision=highest) - jnp.einsum('fbn,bmf->fmn', amp_imag, inv_imag, precision=highest)
    mode_imag = jnp.einsum('fbn,bmf->fmn', amp_real, inv_imag, precision=highest) + jnp.einsum('fbn,bmf->fmn', amp_imag, inv_real, precision=highest)
    return jnp.stack([mode_real, mode_imag])

def reference(snapshots, block_starts, point_slab, slab_weight):
    all_points = snapshots.shape[2]
    piece_size = min(all_points, 4096)
    piece_count = all_points // piece_size
    dft_table, row_sums = make_tables(WIN, NF)
    weights = slab_weight[point_slab]
    root_weight = jnp.sqrt(weights / (0.375 * WIN)).reshape(piece_count, piece_size)
    pieces = jnp.moveaxis(snapshots.reshape(NT, 3, piece_count, piece_size), 2, 0)

    def amplitude_of(series, root_piece):
        spectrum = spectra(series, block_starts, dft_table, row_sums)
        return (spectrum * root_piece).reshape(2, NF, NB, 3 * piece_size)

    def piece_gram(inputs):
        return gram(amplitude_of(inputs[0], inputs[1]))
    sums_real, sums_imag = lax.map(piece_gram, (pieces, root_weight))
    norm_scale = 1.0 / (3.0 * all_points)
    gram_real = lax.optimization_barrier(jnp.sum(sums_real, axis=0)) * norm_scale
    gram_imag = lax.optimization_barrier(jnp.sum(sums_imag, axis=0)) * norm_scale
    upper_real, upper_imag = complex_cholesky(gram_real, gram_imag)
    inv_real, inv_imag = upper_inverse(upper_real, upper_imag)

    def piece_modes(inputs):
        amplitude = amplitude_of(inputs[0], inputs[1])
        return project(amplitude, inv_real, inv_imag).reshape(2, NF, NB, 3, piece_size).astype(jnp.bfloat16)
    modes = lax.map(piece_modes, (pieces, root_weight))
    mode_field = jnp.moveaxis(modes, 0, 4).reshape(2, NF, NB, 3, all_points)
    r_factor = jnp.transpose(jnp.stack([upper_real, upper_imag]), (0, 3, 1, 2))
    return (mode_field, r_factor)
```

```python
import functools
import math

import jax
import jax.numpy as jnp
from jax import lax
from jax.experimental import pallas as pl
from jax.experimental.pallas import tpu as pltpu
from jax.sharding import PartitionSpec as P

WIN = 64
NF = WIN // 2 + 1
ROWS = 32
HALF = ROWS // 2
GROUP = 11
PGROUP = 3
VMEM_LIMIT = 56 * 1024 * 1024


def make_table(length, freq_count):
    steps_time = jnp.arange(length, dtype=jnp.int32)
    freq_index = jnp.arange(freq_count, dtype=jnp.int32)
    phase_index = freq_index[:, None] * steps_time[None, :] % length
    angle_value = 2.0 * math.pi / length * phase_index.astype(jnp.float32)
    window = 0.5 - 0.5 * jnp.cos(2.0 * math.pi / length * steps_time.astype(jnp.float32))
    dft_table = jnp.stack(
        [window[None, :] * jnp.cos(angle_value), -window[None, :] * jnp.sin(angle_value)]
    ).astype(jnp.bfloat16)
    return dft_table


def spectrum_kernel(nt, index_ref, table_ref, root_ref, series_ref, amp_ref, gram_ref, band, sums_ref):
    comps = series_ref.shape[1]
    points = series_ref.shape[3]
    for chunk in range(nt // 128):
        lanes = slice(chunk * 128, (chunk + 1) * 128)
        where = index_ref[:, lanes]
        for j in range(GROUP):
            for k in range(2):
                source = jnp.broadcast_to(table_ref[j, k : k + 1, :], (ROWS, 128))
                values = jnp.take_along_axis(source, where, axis=1, mode="promise_in_bounds")
                row = (2 * j + k) * ROWS
                band[row : row + ROWS, lanes] = values.astype(jnp.bfloat16)
    for j in range(GROUP):
        for k in range(2):
            total = jnp.sum(table_ref[j, k : k + 1, :], axis=1, keepdims=True)
            row = (2 * j + k) * ROWS
            sums_ref[row : row + ROWS, :] = jnp.broadcast_to(total, (ROWS, 128))
    sums = sums_ref[:, 0:1]
    root = root_ref[...]
    ones = jnp.ones((16, nt), jnp.bfloat16)
    for c in range(comps):
        series = series_ref[:, c].reshape(nt, points)
        mean = jnp.dot(ones, series, preferred_element_type=jnp.float32)[0:1] / nt
        raw = jnp.dot(band[...], series, preferred_element_type=jnp.float32)
        amp = (raw - sums * mean) * root
        high = amp.astype(jnp.bfloat16)
        low = (amp - high.astype(jnp.float32)).astype(jnp.bfloat16)
        lanes = slice(c * points, (c + 1) * points)
        amp_ref[:, : 2 * ROWS, lanes] = high.reshape(GROUP, 2 * ROWS, points)
        amp_ref[:, 2 * ROWS :, lanes] = low.reshape(GROUP, 2 * ROWS, points)
    n = 2 * ROWS
    for j in range(GROUP):
        both = amp_ref[j]
        quad = lax.dot_general(both, both, (((1,), (1,)), ((), ())), preferred_element_type=jnp.float32)
        g = quad[:n, :n] + (quad[:n, n:] + quad[n:, :n]) + quad[n:, n:]
        real = g[:ROWS, :ROWS] + g[ROWS:, ROWS:]
        imag = g[:ROWS, ROWS:] - g[ROWS:, :ROWS]
        line = jnp.concatenate([real[:HALF], imag[:HALF], real[HALF:], imag[HALF:]], axis=1)
        gram_ref[:, pl.ds(pl.program_id(0) * GROUP + j, 1), :] = line.reshape(HALF, 1, 4 * ROWS)


def spectrum_call(series, index, table, root):
    parts, comps, times, points = series.shape
    nt = parts * times
    width = comps * points
    n = 2 * ROWS
    return pl.pallas_call(
        functools.partial(spectrum_kernel, nt),
        grid=(NF // GROUP,),
        in_specs=[
            pl.BlockSpec((ROWS, nt), lambda i: (0, 0)),
            pl.BlockSpec((GROUP, 2, 128), lambda i: (i, 0, 0)),
            pl.BlockSpec((1, points), lambda i: (0, 0)),
            pl.BlockSpec(series.shape, lambda i: (0, 0, 0, 0)),
        ],
        out_specs=[
            pl.BlockSpec((GROUP, 2 * n, width), lambda i: (i, 0, 0)),
            pl.BlockSpec((HALF, NF, 4 * ROWS), lambda i: (0, 0, 0)),
        ],
        out_shape=[
            jax.ShapeDtypeStruct((NF, 2 * n, width), jnp.bfloat16),
            jax.ShapeDtypeStruct((HALF, NF, 4 * ROWS), jnp.float32),
        ],
        scratch_shapes=[pltpu.VMEM((GROUP * n, nt), jnp.bfloat16), pltpu.VMEM((GROUP * n, 128), jnp.float32)],
        compiler_params=pltpu.CompilerParams(vmem_limit_bytes=VMEM_LIMIT),
        name="spectrum_gram",
    )(index, table, root, series)


def factor_kernel(nb, scale, gram_ref, r_ref, weight_ref, gr, gi, xr, xi, wide):
    wide[...] = jnp.zeros_like(wide)
    for q in range(HALF):
        wide[:NF, :] = gram_ref[q] * scale
        block = jnp.transpose(wide[...]).reshape(2, 2, ROWS, 128)
        gr[q], gi[q] = block[0, 0], block[0, 1]
        gr[q + HALF], gi[q + HALF] = block[1, 0], block[1, 1]
    shape = (ROWS, ROWS, 128)
    same = lax.broadcasted_iota(jnp.int32, shape, 0) == lax.broadcasted_iota(jnp.int32, shape, 1)
    xr[...] = same.astype(jnp.float32)
    xi[...] = jnp.zeros(shape, jnp.float32)
    used = lax.broadcasted_iota(jnp.int32, (1, 128), 1) < NF
    for i in range(nb):
        low = i // 8 * 8
        top = low + 8
        inverse = 1.0 / jnp.sqrt(jnp.where(used, gr[i, i : i + 1, :], 1.0))
        rr = gr[i, low:, :] * inverse
        ri = gi[i, low:, :] * inverse
        yr = xr[i, :top, :] * inverse
        yi = xi[i, :top, :] * inverse
        if i + 1 < nb:
            lr = gr[i + 1 : nb, i : i + 1, :] * inverse
            li = gi[i + 1 : nb, i : i + 1, :] * inverse
            gr[i + 1 : nb, low:, :] -= lr * rr[None] - li * ri[None]
            gi[i + 1 : nb, low:, :] -= lr * ri[None] + li * rr[None]
            xr[i + 1 : nb, :top, :] -= lr * yr[None] - li * yi[None]
            xi[i + 1 : nb, :top, :] -= lr * yi[None] + li * yr[None]
        column = lax.broadcasted_iota(jnp.int32, rr.shape, 0) + low
        if low:
            gr[i, :low, :] = jnp.zeros((low, 128), jnp.float32)
            gi[i, :low, :] = jnp.zeros((low, 128), jnp.float32)
        gr[i, low:, :] = jnp.where(column >= i, rr, 0.0)
        gi[i, low:, :] = jnp.where(column > i, ri, 0.0)
        xr[i, :top, :] = yr
        xi[i, :top, :] = yi


    r_ref[0] = gr[...]
    r_ref[1] = gi[...]
    for m in range(ROWS):
        real, imag = xr[m], xi[m]
        for k, pair in enumerate(([real, imag], [-imag, real])):
            lines = jnp.transpose(jnp.concatenate(pair + pair, axis=0))
            weight_ref[:, 2 * m + k : 2 * m + k + 1, :] = lines[:NF].reshape(NF, 1, 128)


def factor_call(gram, nb, scale):
    cube = pltpu.VMEM((ROWS, ROWS, 128), jnp.float32)
    return pl.pallas_call(
        functools.partial(factor_kernel, nb, scale),
        out_shape=[
            jax.ShapeDtypeStruct((2, ROWS, ROWS, 128), jnp.float32),
            jax.ShapeDtypeStruct((NF, 2 * ROWS, 4 * ROWS), jnp.float32),
        ],
        scratch_shapes=[cube, cube, cube, cube, pltpu.VMEM((128, 128), jnp.float32)],
        compiler_params=pltpu.CompilerParams(vmem_limit_bytes=VMEM_LIMIT),
        name="factor",
    )(gram)


def project_kernel(weight_ref, amp_ref, out_ref):
    n = 2 * ROWS
    points = out_ref.shape[4]
    for j in range(PGROUP):
        weight = weight_ref[j]
        high = weight.astype(jnp.bfloat16)
        low = (weight - high.astype(jnp.float32)).astype(jnp.bfloat16)
        modes = jnp.dot(high, amp_ref[j], preferred_element_type=jnp.float32)
        modes += jnp.dot(low[:, :n], amp_ref[j, :n, :], preferred_element_type=jnp.float32)
        modes = modes.astype(jnp.bfloat16)
        for c in range(out_ref.shape[2]):
            for m in range(out_ref.shape[1]):
                out_ref[j, m, c] = modes[2 * m : 2 * m + 2, c * points : (c + 1) * points]


def project_call(weight, amp, nb, comps):
    n = 2 * ROWS
    width = amp.shape[2]
    points = width // comps
    return pl.pallas_call(
        project_kernel,
        grid=(NF // PGROUP,),
        in_specs=[
            pl.BlockSpec((PGROUP, n, 2 * n), lambda i: (i, 0, 0)),
            pl.BlockSpec((PGROUP, 2 * n, width), lambda i: (i, 0, 0)),
        ],
        out_specs=pl.BlockSpec((PGROUP, nb, comps, 2, points), lambda i: (i, 0, 0, 0, 0)),
        out_shape=jax.ShapeDtypeStruct((NF, nb, comps, 2, points), jnp.bfloat16),
        compiler_params=pltpu.CompilerParams(vmem_limit_bytes=VMEM_LIMIT),
        name="project",
    )(weight, amp)


def allreduce_kernel(part_ref, out_ref, got1, got2, got3, send1, recv1, send2, recv2, send3, recv3):
    snap = lax.axis_size("snap")
    pts = lax.axis_size("pts")
    ms = lax.axis_index("snap")
    mp = lax.axis_index("pts")
    depth = part_ref.shape[0] // snap
    mesh_id = pl.DeviceIdType.MESH
    barrier = pltpu.get_barrier_semaphore()
    for d in range(1, snap):
        pl.semaphore_signal(barrier, inc=1, device_id=(mp, lax.rem(ms + d, snap)), device_id_type=mesh_id)
    for d in range(1, pts):
        pl.semaphore_signal(barrier, inc=1, device_id=(lax.rem(mp + d, pts), ms), device_id_type=mesh_id)
    pl.semaphore_wait(barrier, snap + pts - 2)

    copies = []
    for d in range(1, snap):
        to = lax.rem(ms + d, snap)
        copies.append(pltpu.make_async_remote_copy(
            src_ref=part_ref.at[pl.ds(to * depth, depth)], dst_ref=got1.at[d], send_sem=send1.at[d], recv_sem=recv1.at[d],
            device_id=(mp, to), device_id_type=mesh_id))
        copies[-1].start()
    total = part_ref[pl.ds(ms * depth, depth)]
    for d in range(1, snap):
        copies[d - 1].wait_recv()
        total = total + got1[d]
    got2[mp] = total
    cross = []
    for d in range(1, pts):
        cross.append(pltpu.make_async_remote_copy(
            src_ref=got2.at[mp], dst_ref=got2.at[mp], send_sem=send2.at[d], recv_sem=recv2.at[d],
            device_id=(lax.rem(mp + d, pts), ms), device_id_type=mesh_id))
        cross[-1].start()
    for copy in cross:
        copy.wait_recv()
    total = got2[0]
    for p in range(1, pts):
        total = total + got2[p]
    got3[ms] = total
    last = []
    for d in range(1, snap):
        last.append(pltpu.make_async_remote_copy(
            src_ref=got3.at[ms], dst_ref=got3.at[ms], send_sem=send3.at[d], recv_sem=recv3.at[d],
            device_id=(mp, lax.rem(ms + d, snap)), device_id_type=mesh_id))
        last[-1].start()
    for copy in last:
        copy.wait_recv()
    for p in range(snap):
        out_ref[p * depth : (p + 1) * depth] = got3[p]
    for copy in copies + cross + last:
        copy.wait_send()


def allreduce_call(part):
    snap = lax.axis_size("snap")
    pts = lax.axis_size("pts")
    slot = (part.shape[0] // snap,) + part.shape[1:]
    dma = pltpu.SemaphoreType.DMA
    return pl.pallas_call(
        allreduce_kernel,
        in_specs=[pl.BlockSpec(memory_space=pltpu.VMEM)],
        out_specs=pl.BlockSpec(memory_space=pltpu.VMEM),
        out_shape=jax.ShapeDtypeStruct(part.shape, part.dtype),
        scratch_shapes=[
            pltpu.VMEM((snap,) + slot, part.dtype),
            pltpu.VMEM((pts,) + slot, part.dtype),
            pltpu.VMEM((snap,) + slot, part.dtype),
            dma((snap,)), dma((snap,)), dma((pts,)), dma((pts,)), dma((snap,)), dma((snap,)),
        ],
        compiler_params=pltpu.CompilerParams(
            collective_id=0, has_side_effects=True, vmem_limit_bytes=VMEM_LIMIT),
        name="gram_sum",
    )(part)


def on_device(snapshots, block_starts, point_slab, slab_weight):
    size = lax.axis_size("snap")
    times, comps, wide_points = snapshots.shape
    points = wide_points // size
    nt = times * size
    nb = block_starts.shape[0]
    all_points = wide_points * lax.axis_size("pts")
    by_owner = jnp.transpose(snapshots.reshape(times, comps, size, points), (2, 1, 0, 3))
    series = lax.all_to_all(by_owner, "snap", split_axis=0, concat_axis=0, tiled=True)

    dft_table = make_table(WIN, NF)
    table = jnp.pad(jnp.moveaxis(dft_table, 0, 1).astype(jnp.float32), ((0, 0), (0, 0), (0, 128 - WIN)))
    starts = jnp.pad(block_starts, (0, ROWS - nb), constant_values=nt)
    offset = jnp.arange(nt, dtype=jnp.int32)[None, :] - starts[:, None]
    index = jnp.where((offset >= 0) & (offset < WIN), offset, WIN)
    slab_ids = jnp.arange(slab_weight.shape[0], dtype=jnp.int32)
    weights = jnp.sum(jnp.where(point_slab[:, None] == slab_ids[None, :], slab_weight[None, :], 0.0), axis=1)
    root = jnp.sqrt(weights / (0.375 * WIN))[None, :]

    amp, part = spectrum_call(series, index, table, root)
    gram = allreduce_call(part)
    r_cube, weight = factor_call(gram, nb, 1.0 / (3.0 * all_points))
    r_factor = jnp.transpose(r_cube[:, :nb, :nb, :NF], (0, 3, 1, 2))
    modes = project_call(weight, amp, nb, comps)
    mode_field = jnp.transpose(modes, (3, 0, 1, 2, 4))
    return (mode_field, r_factor)


def solution(mesh):
    in_specs = (P("snap", None, "pts"), P(), P(("pts", "snap")), P())
    out_specs = (P(None, None, None, None, ("pts", "snap")), P())
    return jax.shard_map(
        on_device, mesh=mesh, in_specs=in_specs, out_specs=out_specs, check_vma=False
    )
```

```python
import functools
import math

import jax
import jax.numpy as jnp
from jax import lax
from jax.experimental import pallas as pl
from jax.experimental.pallas import tpu as pltpu
from jax.sharding import PartitionSpec as P

WIN = 64
NF = WIN // 2 + 1
ROWS = 32
HALF = ROWS // 2
GROUP = 11
PGROUP = 3
VMEM_LIMIT = 56 * 1024 * 1024


def make_table(length, freq_count):
    steps_time = jnp.arange(length, dtype=jnp.int32)
    freq_index = jnp.arange(freq_count, dtype=jnp.int32)
    phase_index = freq_index[:, None] * steps_time[None, :] % length
    angle_value = 2.0 * math.pi / length * phase_index.astype(jnp.float32)
    window = 0.5 - 0.5 * jnp.cos(2.0 * math.pi / length * steps_time.astype(jnp.float32))
    dft_table = jnp.stack(
        [window[None, :] * jnp.cos(angle_value), -window[None, :] * jnp.sin(angle_value)]
    ).astype(jnp.bfloat16)
    return dft_table


def band_kernel(nt, index_ref, table_ref, band_ref, sums_ref):
    for j in range(GROUP):
        for k in range(2):
            line = table_ref[j, k : k + 1, :]
            source = jnp.broadcast_to(line, (ROWS, 128))
            row = (2 * j + k) * ROWS
            for chunk in range(nt // 128):
                lanes = slice(chunk * 128, (chunk + 1) * 128)
                values = jnp.take_along_axis(source, index_ref[:, lanes], axis=1, mode="promise_in_bounds")
                band_ref[row : row + ROWS, lanes] = values.astype(jnp.bfloat16)
            total = jnp.sum(line, axis=1, keepdims=True)
            sums_ref[row : row + ROWS, :] = jnp.broadcast_to(total, (ROWS, 128))


def band_call(index, table):
    nt = index.shape[1]
    rows = GROUP * 2 * ROWS
    return pl.pallas_call(
        functools.partial(band_kernel, nt),
        grid=(NF // GROUP,),
        in_specs=[
            pl.BlockSpec((ROWS, nt), lambda i: (0, 0)),
            pl.BlockSpec((GROUP, 2, 128), lambda i: (i, 0, 0)),
        ],
        out_specs=[
            pl.BlockSpec((rows, nt), lambda i: (i, 0)),
            pl.BlockSpec((rows, 128), lambda i: (i, 0)),
        ],
        out_shape=[
            jax.ShapeDtypeStruct((NF * 2 * ROWS, nt), jnp.bfloat16),
            jax.ShapeDtypeStruct((NF * 2 * ROWS, 128), jnp.float32),
        ],
        compiler_params=pltpu.CompilerParams(vmem_limit_bytes=VMEM_LIMIT),
        name="band",
    )(index, table)


def spectrum_kernel(
    band_ref, sums_ref, root_ref, snap_ref, amp_ref, gram_ref, series, amp, send, recv, own, store
):
    snap = lax.axis_size("snap")
    ms = lax.axis_index("snap")
    mp = lax.axis_index("pts")
    mesh_id = pl.DeviceIdType.MESH
    comps, _, times, points = series.shape
    nt = snap * times
    n = 2 * ROWS
    barrier = pltpu.get_barrier_semaphore()
    for d in range(1, snap):
        pl.semaphore_signal(barrier, inc=1, device_id=(mp, lax.rem(ms + d, snap)), device_id_type=mesh_id)
    pl.semaphore_wait(barrier, snap - 1)

    kept, sent, stored = [], [], []
    for c in range(comps):
        mine = pl.ds(pl.multiple_of(ms * points, points), points)
        kept.append(pltpu.make_async_copy(snap_ref.at[c, :, mine], series.at[c, ms], own.at[c]))
        kept[c].start()
        sent.append([])
        for d in range(1, snap):
            to = lax.rem(ms + d, snap)
            theirs = pl.ds(pl.multiple_of(to * points, points), points)
            copy = pltpu.make_async_remote_copy(
                src_ref=snap_ref.at[c, :, theirs], dst_ref=series.at[c, ms],
                send_sem=send.at[c, d], recv_sem=recv.at[c, d],
                device_id=(mp, to), device_id_type=mesh_id)
            copy.start()
            sent[c].append(copy)

    gram_ref[...] = jnp.zeros_like(gram_ref)
    root = root_ref[...]
    ones = jnp.ones((16, nt), jnp.bfloat16)
    for c in range(comps):
        kept[c].wait()
        for copy in sent[c]:
            copy.wait_recv()
        lanes = slice(c * points, (c + 1) * points)
        mean = jnp.dot(ones, series[c].reshape(nt, points), preferred_element_type=jnp.float32)[0:1] / nt

        def group_step(g, _):
            rows = pl.ds(pl.multiple_of(g * (GROUP * n), GROUP * n), GROUP * n)
            raw = jnp.dot(band_ref[rows, :], series[c].reshape(nt, points), preferred_element_type=jnp.float32)
            value = (raw - sums_ref[rows, 0:1] * mean) * root
            high = value.astype(jnp.bfloat16)
            low = (value - high.astype(jnp.float32)).astype(jnp.bfloat16)
            amp[pl.ds(g * GROUP, GROUP), :n, lanes] = high.reshape(GROUP, n, points)
            amp[pl.ds(g * GROUP, GROUP), n:, lanes] = low.reshape(GROUP, n, points)
            for j in range(GROUP):
                f = g * GROUP + j
                both = amp[f, :, lanes]
                quad = lax.dot_general(both, both, (((1,), (1,)), ((), ())), preferred_element_type=jnp.float32)
                full = quad[:n, :n] + (quad[:n, n:] + quad[n:, :n]) + quad[n:, n:]
                real = full[:ROWS, :ROWS] + full[ROWS:, ROWS:]
                imag = full[:ROWS, ROWS:] - full[ROWS:, :ROWS]
                line = jnp.concatenate([real[:HALF], imag[:HALF], real[HALF:], imag[HALF:]], axis=1)
                gram_ref[:, pl.ds(f, 1), :] += line.reshape(HALF, 1, 4 * ROWS)
            return 0

        lax.fori_loop(0, NF // GROUP, group_step, 0)
        stored.append(pltpu.make_async_copy(amp.at[:, :, lanes], amp_ref.at[:, :, lanes], store.at[c]))
        stored[c].start()
    for c in range(comps):
        stored[c].wait()
        for copy in sent[c]:
            copy.wait_send()


def spectrum_call(snapshots, band, sums, root):
    comps, times, wide_points = snapshots.shape
    snap = lax.axis_size("snap")
    points = wide_points // snap
    width = comps * points
    n = 2 * ROWS
    dma = pltpu.SemaphoreType.DMA
    vmem = pl.BlockSpec(memory_space=pltpu.VMEM)
    hbm = pl.BlockSpec(memory_space=pl.ANY)
    return pl.pallas_call(
        spectrum_kernel,
        in_specs=[vmem, vmem, vmem, hbm],
        out_specs=[hbm, vmem],
        out_shape=[
            jax.ShapeDtypeStruct((NF, 2 * n, width), jnp.bfloat16),
            jax.ShapeDtypeStruct((HALF, NF, 4 * ROWS), jnp.float32),
        ],
        scratch_shapes=[
            pltpu.VMEM((comps, snap, times, points), jnp.bfloat16),
            pltpu.VMEM((NF, 2 * n, width), jnp.bfloat16),
            dma((comps, snap)), dma((comps, snap)), dma((comps,)), dma((comps,)),
        ],
        compiler_params=pltpu.CompilerParams(
            collective_id=1, has_side_effects=True, vmem_limit_bytes=VMEM_LIMIT),
        name="spectrum_gram",
    )(band, sums, root, snapshots)


def factor_kernel(nb, scale, gram_ref, r_ref, weight_ref, gr, gi, xr, xi, wide):
    wide[...] = jnp.zeros_like(wide)
    for q in range(HALF):
        wide[:NF, :] = gram_ref[q] * scale
        block = jnp.transpose(wide[...]).reshape(2, 2, ROWS, 128)
        gr[q], gi[q] = block[0, 0], block[0, 1]
        gr[q + HALF], gi[q + HALF] = block[1, 0], block[1, 1]
    shape = (ROWS, ROWS, 128)
    same = lax.broadcasted_iota(jnp.int32, shape, 0) == lax.broadcasted_iota(jnp.int32, shape, 1)
    xr[...] = same.astype(jnp.float32)
    xi[...] = jnp.zeros(shape, jnp.float32)
    used = lax.broadcasted_iota(jnp.int32, (1, 128), 1) < NF
    for i in range(nb):
        low = i // 8 * 8
        top = low + 8
        inverse = 1.0 / jnp.sqrt(jnp.where(used, gr[i, i : i + 1, :], 1.0))
        rr = gr[i, low:, :] * inverse
        ri = gi[i, low:, :] * inverse
        yr = xr[i, :top, :] * inverse
        yi = xi[i, :top, :] * inverse
        if i + 1 < nb:
            lr = gr[i + 1 : nb, i : i + 1, :] * inverse
            li = gi[i + 1 : nb, i : i + 1, :] * inverse
            gr[i + 1 : nb, low:, :] -= lr * rr[None] - li * ri[None]
            gi[i + 1 : nb, low:, :] -= lr * ri[None] + li * rr[None]
            xr[i + 1 : nb, :top, :] -= lr * yr[None] - li * yi[None]
            xi[i + 1 : nb, :top, :] -= lr * yi[None] + li * yr[None]
        column = lax.broadcasted_iota(jnp.int32, rr.shape, 0) + low
        if low:
            gr[i, :low, :] = jnp.zeros((low, 128), jnp.float32)
            gi[i, :low, :] = jnp.zeros((low, 128), jnp.float32)
        gr[i, low:, :] = jnp.where(column >= i, rr, 0.0)
        gi[i, low:, :] = jnp.where(column > i, ri, 0.0)
        xr[i, :top, :] = yr
        xi[i, :top, :] = yi


    r_ref[0] = gr[...]
    r_ref[1] = gi[...]
    for m in range(ROWS):
        real, imag = xr[m], xi[m]
        for k, pair in enumerate(([real, imag], [-imag, real])):
            lines = jnp.transpose(jnp.concatenate(pair + pair, axis=0))
            weight_ref[:, 2 * m + k : 2 * m + k + 1, :] = lines[:NF].reshape(NF, 1, 128)


def factor_call(gram, nb, scale):
    cube = pltpu.VMEM((ROWS, ROWS, 128), jnp.float32)
    return pl.pallas_call(
        functools.partial(factor_kernel, nb, scale),
        out_shape=[
            jax.ShapeDtypeStruct((2, ROWS, ROWS, 128), jnp.float32),
            jax.ShapeDtypeStruct((NF, 2 * ROWS, 4 * ROWS), jnp.float32),
        ],
        scratch_shapes=[cube, cube, cube, cube, pltpu.VMEM((128, 128), jnp.float32)],
        compiler_params=pltpu.CompilerParams(vmem_limit_bytes=VMEM_LIMIT),
        name="factor",
    )(gram)


def project_kernel(weight_ref, amp_ref, out_ref):
    n = 2 * ROWS
    points = out_ref.shape[4]
    for j in range(PGROUP):
        weight = weight_ref[j]
        high = weight.astype(jnp.bfloat16)
        low = (weight - high.astype(jnp.float32)).astype(jnp.bfloat16)
        modes = jnp.dot(high, amp_ref[j], preferred_element_type=jnp.float32)
        modes += jnp.dot(low[:, :n], amp_ref[j, :n, :], preferred_element_type=jnp.float32)
        modes = modes.astype(jnp.bfloat16)
        for c in range(out_ref.shape[2]):
            for m in range(out_ref.shape[1]):
                out_ref[j, m, c] = modes[2 * m : 2 * m + 2, c * points : (c + 1) * points]


def project_call(weight, amp, nb, comps):
    n = 2 * ROWS
    width = amp.shape[2]
    points = width // comps
    return pl.pallas_call(
        project_kernel,
        grid=(NF // PGROUP,),
        in_specs=[
            pl.BlockSpec((PGROUP, n, 2 * n), lambda i: (i, 0, 0)),
            pl.BlockSpec((PGROUP, 2 * n, width), lambda i: (i, 0, 0)),
        ],
        out_specs=pl.BlockSpec((PGROUP, nb, comps, 2, points), lambda i: (i, 0, 0, 0, 0)),
        out_shape=jax.ShapeDtypeStruct((NF, nb, comps, 2, points), jnp.bfloat16),
        compiler_params=pltpu.CompilerParams(vmem_limit_bytes=VMEM_LIMIT),
        name="project",
    )(weight, amp)


def allreduce_kernel(part_ref, out_ref, got1, got2, got3, send1, recv1, send2, recv2, send3, recv3):
    snap = lax.axis_size("snap")
    pts = lax.axis_size("pts")
    ms = lax.axis_index("snap")
    mp = lax.axis_index("pts")
    depth = part_ref.shape[0] // snap
    mesh_id = pl.DeviceIdType.MESH
    barrier = pltpu.get_barrier_semaphore()
    for d in range(1, snap):
        pl.semaphore_signal(barrier, inc=1, device_id=(mp, lax.rem(ms + d, snap)), device_id_type=mesh_id)
    for d in range(1, pts):
        pl.semaphore_signal(barrier, inc=1, device_id=(lax.rem(mp + d, pts), ms), device_id_type=mesh_id)
    pl.semaphore_wait(barrier, snap + pts - 2)

    copies = []
    for d in range(1, snap):
        to = lax.rem(ms + d, snap)
        copies.append(pltpu.make_async_remote_copy(
            src_ref=part_ref.at[pl.ds(to * depth, depth)], dst_ref=got1.at[d], send_sem=send1.at[d], recv_sem=recv1.at[d],
            device_id=(mp, to), device_id_type=mesh_id))
        copies[-1].start()
    total = part_ref[pl.ds(ms * depth, depth)]
    for d in range(1, snap):
        copies[d - 1].wait_recv()
        total = total + got1[d]
    got2[mp] = total
    cross = []
    for d in range(1, pts):
        cross.append(pltpu.make_async_remote_copy(
            src_ref=got2.at[mp], dst_ref=got2.at[mp], send_sem=send2.at[d], recv_sem=recv2.at[d],
            device_id=(lax.rem(mp + d, pts), ms), device_id_type=mesh_id))
        cross[-1].start()
    for copy in cross:
        copy.wait_recv()
    total = got2[0]
    for p in range(1, pts):
        total = total + got2[p]
    got3[ms] = total
    last = []
    for d in range(1, snap):
        last.append(pltpu.make_async_remote_copy(
            src_ref=got3.at[ms], dst_ref=got3.at[ms], send_sem=send3.at[d], recv_sem=recv3.at[d],
            device_id=(mp, lax.rem(ms + d, snap)), device_id_type=mesh_id))
        last[-1].start()
    for copy in last:
        copy.wait_recv()
    for p in range(snap):
        out_ref[p * depth : (p + 1) * depth] = got3[p]
    for copy in copies + cross + last:
        copy.wait_send()


def allreduce_call(part):
    snap = lax.axis_size("snap")
    pts = lax.axis_size("pts")
    slot = (part.shape[0] // snap,) + part.shape[1:]
    dma = pltpu.SemaphoreType.DMA
    return pl.pallas_call(
        allreduce_kernel,
        in_specs=[pl.BlockSpec(memory_space=pltpu.VMEM)],
        out_specs=pl.BlockSpec(memory_space=pltpu.VMEM),
        out_shape=jax.ShapeDtypeStruct(part.shape, part.dtype),
        scratch_shapes=[
            pltpu.VMEM((snap,) + slot, part.dtype),
            pltpu.VMEM((pts,) + slot, part.dtype),
            pltpu.VMEM((snap,) + slot, part.dtype),
            dma((snap,)), dma((snap,)), dma((pts,)), dma((pts,)), dma((snap,)), dma((snap,)),
        ],
        compiler_params=pltpu.CompilerParams(
            collective_id=0, has_side_effects=True, vmem_limit_bytes=VMEM_LIMIT),
        name="gram_sum",
    )(part)


def on_device(snapshots, block_starts, point_slab, slab_weight):
    size = lax.axis_size("snap")
    times, comps, wide_points = snapshots.shape
    points = wide_points // size
    nt = times * size
    nb = block_starts.shape[0]
    all_points = wide_points * lax.axis_size("pts")
    dft_table = make_table(WIN, NF)
    table = jnp.pad(jnp.moveaxis(dft_table, 0, 1).astype(jnp.float32), ((0, 0), (0, 0), (0, 128 - WIN)))
    starts = jnp.pad(block_starts, (0, ROWS - nb), constant_values=nt)
    offset = jnp.arange(nt, dtype=jnp.int32)[None, :] - starts[:, None]
    index = jnp.where((offset >= 0) & (offset < WIN), offset, WIN)
    slab_ids = jnp.arange(slab_weight.shape[0], dtype=jnp.int32)
    weights = jnp.sum(jnp.where(point_slab[:, None] == slab_ids[None, :], slab_weight[None, :], 0.0), axis=1)
    root = jnp.sqrt(weights / (0.375 * WIN))[None, :]

    band, sums = band_call(index, table)
    amp, part = spectrum_call(jnp.transpose(snapshots, (1, 0, 2)), band, sums, root)
    gram = allreduce_call(part)
    r_cube, weight = factor_call(gram, nb, 1.0 / (3.0 * all_points))
    r_factor = jnp.transpose(r_cube[:, :nb, :nb, :NF], (0, 3, 1, 2))
    modes = project_call(weight, amp, nb, comps)
    mode_field = jnp.transpose(modes, (3, 0, 1, 2, 4))
    return (mode_field, r_factor)


def solution(mesh):
    in_specs = (P("snap", None, "pts"), P(), P(("pts", "snap")), P())
    out_specs = (P(None, None, None, None, ("pts", "snap")), P())
    return jax.shard_map(
        on_device, mesh=mesh, in_specs=in_specs, out_specs=out_specs, check_vma=False
    )
```
